32 devices in a mesh: inst: 2 (over y), row: 4 (over x, core), col: 4 (over z).
Axes of the slice: x: 2, y: 2, z: 4, core: 2. Of those that a mesh axis runs over, the one named last changes fastest.
Arguments:
- block_values: bfloat16 [8, 4, 32, 128, 128], P(('inst', 'row'), 'col'), parts along dimension 0, may hold values from -0.125 to 0.125
- block_rows: int32 [8, 4, 32], P(('inst', 'row'), 'col'), parts along dimension 0, may hold values from 0 to 7, as said below
- block_cols: int32 [8, 4, 32], P(('inst', 'row'), 'col'), parts along dimension 0, may hold values from 0 to 7, as said below
- block_count: int32 [8, 4], P(('inst', 'row'), 'col'), parts along dimension 0, may hold values from 4 to 32, as said below
- scenario_live: int32 [8192], P(('inst', 'row')), parts along dimension 0, may hold values 0 or 1
- demand: float32 [8192, 256], P(('inst', 'row'), 'col'), parts along dimension 0, may hold values from -6 to 6
- path_cost: float32 [8192], P(('inst', 'col')), parts along dimension 0, may hold values from -6 to 6
- upper_bound: float32 [8192], P(('inst', 'col')), parts along dimension 0, may hold values from 0.5 to 2
- primal_start: float32 [8192, 256], P(('inst', 'col'), 'row'), parts along dimension 0, may hold values from 0 to 2
- dual_start: float32 [8192, 256], P(('inst', 'row'), 'col'), parts along dimension 0, may hold values from 0 to 1
Outputs:
- primal: float32 [8192, 256], P(('inst', 'col'), 'row'), parts along dimension 0
- dual: float32 [8192, 256], P(('inst', 'row'), 'col'), parts along dimension 0
The draws below stay inside these ranges and needn't reach their ends.
There are 2 independent parts, one for each index of `inst`. The reference program is written for one: setup_inputs(seed, part) draws one part's arguments, and reference() takes and returns one part's arrays. A program takes and returns all parts, laid end to end along the dimension named above; each array names one. Nothing has to cross between parts.
Inputs may be any that keep to these rules, and one draw needn't show every extreme that they name: `block_rows`: within a tile, the slots hold different (block row, block column) pairs; slots at or past the tile's block_count are ignored. `block_cols`: within a tile, the slots hold different (block row, block column) pairs; slots at or past the tile's block_count are ignored. `block_count`: some tile holds exactly 32 blocks.
All inputs are finite; a program needn't handle non-finite values. No bound on the sum of `scenario_live` on one device may be relied on, other than what follows from the above.
Results may differ from the reference program's by a relative error of at most 0.0011.
Values may be sent and summed in bfloat16 or wider, within the bound.
A program may use at most 64 MiB of HBM per device.

```python
import math
import jax
import jax.numpy as jnp
from jax import lax

BLK = 128
RHS = 256
BR_DEV = 8
BC_DEV = 8
KMAX = 32
ITERS = 4
NCON = 4096
NVAR = 4096
N_ROW = 4
N_COL = 4


def block_pattern(key):
    tiles = N_ROW * N_COL
    tile_keys = jax.random.split(jax.random.fold_in(key, 11), tiles)
    orders = jax.vmap(lambda one_key: jax.random.permutation(one_key, BR_DEV * BC_DEV))(tile_keys)[:, :KMAX]
    orders = orders.astype(jnp.int32)
    filled = jax.random.randint(jax.random.fold_in(key, 12), (tiles,), max(1, KMAX // 8), KMAX + 1).astype(jnp.int32)
    fullest = jax.random.randint(jax.random.fold_in(key, 13), (), 0, tiles).astype(jnp.int32)
    filled = jnp.where(jnp.arange(tiles, dtype=jnp.int32) == fullest, KMAX, filled).astype(jnp.int32)
    row_ids = (orders // BC_DEV).reshape(N_ROW, N_COL, KMAX)
    col_ids = (orders % BC_DEV).reshape(N_ROW, N_COL, KMAX)
    return (row_ids, col_ids, filled.reshape(N_ROW, N_COL))


def draw_block_rows(key, part):
    pattern = block_pattern(key)
    return pattern[0].astype(jnp.int32)


def draw_block_cols(key, part):
    pattern = block_pattern(key)
    return pattern[1].astype(jnp.int32)


def draw_block_count(key, part):
    pattern = block_pattern(key)
    return pattern[2].astype(jnp.int32)


def touch_ends(values, own_key, least, top_value):
    longest = values.shape.index(max(values.shape))
    spots = []
    for shift in (0, 1):
        where = [jax.random.randint(jax.random.fold_in(own_key, axis), (), 0, length) for axis, length in enumerate(values.shape)]
        where[longest] = (where[longest] + shift) % values.shape[longest]
        spots.append(tuple(where))
    return values.at[spots[0]].set(least).at[spots[1]].set(top_value)


def level_of(own_key, extent, cuts, smallest, high):
    factor_of, own = 1.0, jax.random.fold_in(own_key, 6)
    for dim, blocks in cuts:
        heights = jnp.exp(jax.random.uniform(jax.random.fold_in(own, dim), (blocks,), jnp.float32, smallest / len(cuts), high / len(cuts)))
        factor_of = factor_of * jnp.repeat(heights, extent[dim] // blocks).reshape([-1 if axis == dim else 1 for axis in range(len(extent))])
    return factor_of


def gaussian(stream_key, dims, width, reach, cuts=(), held_as=jnp.bfloat16):
    values = width * jax.random.normal(stream_key, dims, jnp.float32)
    if cuts:
        values = values * level_of(stream_key, dims, cuts, -0.22, 0.18)
    return jnp.clip(values, -reach, reach).astype(held_as)


def setup_inputs(seed: int = 0, part: int = 0) -> dict:
    key_list = jax.random.split(jax.random.key(seed), 11)
    part_keys = jax.random.split(jax.random.fold_in(key_list[10], part), 11)
    return {
        "block_values": gaussian(part_keys[0], (N_ROW, N_COL, KMAX, BLK, BLK), (N_COL * BC_DEV * BLK // 2) ** -0.5, 0.125, ((0, 4), (1, 4))),
        "block_rows": draw_block_rows(jax.random.fold_in(jax.random.fold_in(key_list[10], part), 71), part),
        "block_cols": draw_block_cols(jax.random.fold_in(jax.random.fold_in(key_list[10], part), 71), part),
        "block_count": draw_block_count(jax.random.fold_in(jax.random.fold_in(key_list[10], part), 71), part),
        "scenario_live": touch_ends((jax.random.randint(part_keys[4], (NCON,), 0, 4) < 3).astype(jnp.int32), jax.random.fold_in(part_keys[4], 1), 0, 1),
        "demand": gaussian(part_keys[5], (NCON, RHS), 1.0, 6.0, ((0, 4), (1, 4)), jnp.float32),
        "path_cost": gaussian(part_keys[6], (NVAR,), 1.0, 6.0, ((0, 4),), jnp.float32),
        "upper_bound": jnp.clip(jnp.exp(math.log(2.0) - 1.3862944 * jax.random.uniform(part_keys[7], (NVAR,), jnp.float32) ** level_of(part_keys[7], (NVAR,), ((0, 4),), -0.2, 0.2)), 0.5, 2.0),
        "primal_start": jnp.clip(2.0 * jax.random.uniform(part_keys[8], (NVAR, RHS), jnp.float32) ** level_of(part_keys[8], (NVAR, RHS), ((0, 4), (1, 4)), -0.2, 0.2), 0.0, 2.0),
        "dual_start": jnp.clip(1.0 * jax.random.uniform(part_keys[9], (NCON, RHS), jnp.float32) ** level_of(part_keys[9], (NCON, RHS), ((0, 4), (1, 4)), -0.2, 0.2), 0.0, 1.0),
    }


primal_step = 0.4
dual_step = 0.4


def forward_tile(values, row_ids, col_ids, filled, source, row_blocks):
    block_size = values.shape[1]
    columns = source.shape[1]
    blocks = source.reshape(-1, block_size, columns)
    picked = blocks[col_ids]
    product = jnp.einsum("kij,kjr->kir", values.astype(jnp.float32), picked.astype(jnp.float32), precision=lax.Precision.HIGHEST)
    slots = jnp.arange(row_ids.shape[0], dtype=jnp.int32)
    chosen = ((row_ids[None, :] == jnp.arange(row_blocks, dtype=jnp.int32)[:, None]) & (slots < filled)[None, :]).astype(jnp.float32)
    result = jnp.einsum("nk,kir->nir", chosen, product, precision=lax.Precision.HIGHEST)
    return result.reshape(row_blocks * block_size, columns)


def transpose_tile(values, row_ids, col_ids, filled, source, col_blocks):
    block_size = values.shape[1]
    columns = source.shape[1]
    blocks = source.reshape(-1, block_size, columns)
    picked = blocks[row_ids]
    product = jnp.einsum("kij,kir->kjr", values.astype(jnp.float32), picked.astype(jnp.float32), precision=lax.Precision.HIGHEST)
    slots = jnp.arange(col_ids.shape[0], dtype=jnp.int32)
    chosen = ((col_ids[None, :] == jnp.arange(col_blocks, dtype=jnp.int32)[:, None]) & (slots < filled)[None, :]).astype(jnp.float32)
    result = jnp.einsum("nk,kjr->njr", chosen, product, precision=lax.Precision.HIGHEST)
    return result.reshape(col_blocks * block_size, columns)


def reference(block_values, block_rows, block_cols, block_count, scenario_live, demand, path_cost, upper_bound, primal_start, dual_start):
    primal = primal_start
    dual = dual_start
    live = scenario_live.astype(jnp.float32)[:, None]

    def apply_matrix(extrapolated):
        sources = extrapolated.reshape(N_COL, BC_DEV * BLK, RHS)

        def one_row(tiles):
            values, row_ids, col_ids, filled = tiles
            parts = jax.vmap(lambda v, a, b, f, s: forward_tile(v, a, b, f, s, BR_DEV))(values, row_ids, col_ids, filled, sources)
            return jnp.sum(parts, axis=0)

        loads = lax.map(one_row, (block_values, block_rows, block_cols, block_count))
        return loads.reshape(N_ROW * BR_DEV * BLK, RHS)

    def apply_transpose(dual_low):
        sources = dual_low.reshape(N_ROW, BR_DEV * BLK, RHS)

        def one_column(tiles):
            values, row_ids, col_ids, filled = tiles
            parts = jax.vmap(lambda v, a, b, f, s: transpose_tile(v, a, b, f, s, BC_DEV))(values, row_ids, col_ids, filled, sources)
            return jnp.sum(parts, axis=0)

        tiles = (jnp.swapaxes(block_values, 0, 1), jnp.swapaxes(block_rows, 0, 1), jnp.swapaxes(block_cols, 0, 1), jnp.swapaxes(block_count, 0, 1))
        lifted = lax.map(one_column, tiles)
        return lifted.reshape(N_COL * BC_DEV * BLK, RHS)

    for step in range(ITERS):
        dual_low = dual.astype(jnp.bfloat16)
        lifted = apply_transpose(dual_low)
        next_primal = jnp.minimum(jnp.maximum(primal - primal_step * (path_cost[:, None] - lifted), 0.0), upper_bound[:, None])
        extrapolated = (2.0 * next_primal - primal).astype(jnp.bfloat16)
        loads = apply_matrix(extrapolated)
        dual = live * jnp.maximum(dual + dual_step * (demand - loads), 0.0)
        primal = next_primal
    return primal, dual
```

```python
import functools

import jax
import jax.numpy as jnp
from jax import lax
from jax.experimental import pallas as pl
from jax.experimental.pallas import tpu as pltpu
from jax.sharding import PartitionSpec as P

ITERS = 4

primal_step = 0.4
dual_step = 0.4

MESH = pl.DeviceIdType.MESH
BF16 = jnp.bfloat16
F32 = jnp.float32


def kernel(
    n_row,
    n_col,
    chains,
    row_blocks,
    col_blocks,
    slot_ref,
    mask_ref,
    values_ref,
    live_ref,
    demand_ref,
    cost_ref,
    bound_ref,
    primal_in,
    dual_in,
    primal_ref,
    dual_ref,
    matrix,
    dual_all,
    lift_part,
    lift_out,
    lift_in,
    flow_all,
    load_part,
    load_out,
    load_in,
    dual_sems,
    lift_sems,
    flow_sems,
    load_sems,
):
    row = lax.axis_index("row")
    col = lax.axis_index("col")
    block = values_ref.shape[1]
    rows_g = primal_in.shape[1]
    cols_g = dual_in.shape[1]

    def peer(axis, d):
        me, n = (row, n_row) if axis == "row" else (col, n_col)
        return lax.rem(me + d, n)

    barrier = pltpu.get_barrier_semaphore()
    for axis, n in (("row", n_row), ("col", n_col)):
        for d in range(1, n):
            pl.semaphore_signal(
                barrier, inc=1, device_id={axis: peer(axis, d)}, device_id_type=MESH
            )

    def copies(axis, n, source, target, sems, h, gather):
        me = row if axis == "row" else col
        made = []
        for d in range(1, n):
            to = peer(axis, d)
            made.append(
                pltpu.make_async_remote_copy(
                    src_ref=source.at[h, me if gather else to],
                    dst_ref=target.at[h, me],
                    send_sem=sems.at[0, h, d - 1],
                    recv_sem=sems.at[1, h, d - 1],
                    device_id={axis: to},
                    device_id_type=MESH,
                )
            )
        return made

    dual_cp = [
        copies("col", n_col, dual_all, dual_all, dual_sems, h, True) for h in range(chains)
    ]
    lift_cp = [
        copies("row", n_row, lift_out, lift_in, lift_sems, h, False) for h in range(chains)
    ]
    flow_cp = [
        copies("row", n_row, flow_all, flow_all, flow_sems, h, True) for h in range(chains)
    ]
    load_cp = [
        copies("col", n_col, load_out, load_in, load_sems, h, False) for h in range(chains)
    ]

    def send(made):
        for one in made:
            one.start()

    def settle(made):
        for one in made:
            one.wait()

    for h in range(chains):
        primal_ref[h] = primal_in[h]
        dual_ref[h] = dual_in[h]
        dual_all[h, col] = dual_in[h].astype(BF16)
    pl.semaphore_wait(barrier, n_row + n_col - 2)
    for h in range(chains):
        send(dual_cp[h])

    for r in range(row_blocks):
        for c in range(col_blocks):
            at = r * col_blocks + c
            placed = values_ref[slot_ref[at]].astype(F32) * mask_ref[at]
            matrix[r * block : (r + 1) * block, c * block : (c + 1) * block] = placed.astype(BF16)

    def lift(h):
        settle(dual_cp[h])
        source = dual_all[h].reshape(n_col * cols_g, matrix.shape[0])
        part = jnp.dot(source, matrix[...], preferred_element_type=F32)
        part = part.reshape(n_row, rows_g, matrix.shape[1])
        lift_part[h] = part
        lift_out[h] = part.astype(BF16)
        send(lift_cp[h])

    def move_primal(h):
        settle(lift_cp[h])
        lifted = lift_part[h, row]
        for d in range(1, n_row):
            lifted = lifted + lift_in[h, lax.rem(row + n_row - d, n_row)].astype(F32)
        primal = primal_ref[h]
        following = jnp.minimum(
            jnp.maximum(primal - primal_step * (cost_ref[...] - lifted), 0.0), bound_ref[...]
        )
        primal_ref[h] = following
        flow_all[h, row] = (2.0 * following - primal).astype(BF16)
        send(flow_cp[h])

    def load(h):
        settle(flow_cp[h])
        source = flow_all[h].reshape(n_row * rows_g, matrix.shape[1])
        part = lax.dot_general(
            source, matrix[...], (((1,), (1,)), ((), ())), preferred_element_type=F32
        )
        part = part.reshape(n_col, cols_g, matrix.shape[0])
        load_part[h] = part
        load_out[h] = part.astype(BF16)
        send(load_cp[h])

    def move_dual(h, step):
        settle(load_cp[h])
        loads = load_part[h, col]
        for d in range(1, n_col):
            loads = loads + load_in[h, lax.rem(col + n_col - d, n_col)].astype(F32)
        dual = live_ref[...] * jnp.maximum(
            dual_ref[h] + dual_step * (demand_ref[h] - loads), 0.0
        )
        dual_ref[h] = dual
        dual_all[h, col] = dual.astype(BF16)

        @pl.when(step < ITERS - 1)
        def _():
            send(dual_cp[h])

    def one_step(step, carry):
        if chains == 2:
            lift(0)
            move_primal(0)
            lift(1)
            load(0)
            move_primal(1)
            load(1)
            move_dual(0, step)
            move_dual(1, step)
        else:
            for h in range(chains):
                lift(h)
            for h in range(chains):
                move_primal(h)
            for h in range(chains):
                load(h)
            for h in range(chains):
                move_dual(h, step)
        return carry

    lax.fori_loop(0, ITERS, one_step, 0)


def on_device(
    n_row,
    n_col,
    block_values,
    block_rows,
    block_cols,
    block_count,
    scenario_live,
    demand,
    path_cost,
    upper_bound,
    primal_start,
    dual_start,
):
    values = block_values[0, 0]
    slots, block_size = values.shape[0], values.shape[1]
    n_con, cols_g = dual_start.shape
    n_var, rows_g = primal_start.shape
    row_blocks = n_con // block_size
    col_blocks = n_var // block_size
    numbers = jnp.arange(slots, dtype=jnp.int32)
    place = block_rows[0, 0] * col_blocks + block_cols[0, 0]
    hit = (place[None, :] == jnp.arange(row_blocks * col_blocks, dtype=jnp.int32)[:, None]) & (
        numbers < block_count[0, 0]
    )[None, :]
    slot = jnp.sum(jnp.where(hit, numbers[None, :], 0), axis=1)
    mask = jnp.sum(jnp.where(hit, 1.0, 0.0), axis=1)

    chains = 2 if n_row == n_col and cols_g == rows_g and cols_g % 32 == 0 else 1
    cg, rg = cols_g // chains, rows_g // chains

    def turned(array):
        return array.T.reshape(chains, array.shape[1] // chains, array.shape[0])

    vmem = pl.BlockSpec(memory_space=pltpu.VMEM)
    smem = pl.BlockSpec(memory_space=pltpu.SMEM)
    primal, dual = pl.pallas_call(
        functools.partial(kernel, n_row, n_col, chains, row_blocks, col_blocks),
        out_shape=(
            jax.ShapeDtypeStruct((chains, rg, n_var), F32),
            jax.ShapeDtypeStruct((chains, cg, n_con), F32),
        ),
        in_specs=[smem, smem] + [vmem] * 7,
        out_specs=(vmem, vmem),
        scratch_shapes=[
            pltpu.VMEM((n_con, n_var), BF16),
            pltpu.VMEM((chains, n_col, cg, n_con), BF16),
            pltpu.VMEM((chains, n_row, rg, n_var), F32),
            pltpu.VMEM((chains, n_row, rg, n_var), BF16),
            pltpu.VMEM((chains, n_row, rg, n_var), BF16),
            pltpu.VMEM((chains, n_row, rg, n_var), BF16),
            pltpu.VMEM((chains, n_col, cg, n_con), F32),
            pltpu.VMEM((chains, n_col, cg, n_con), BF16),
            pltpu.VMEM((chains, n_col, cg, n_con), BF16),
            pltpu.SemaphoreType.DMA((2, chains, n_col - 1)),
            pltpu.SemaphoreType.DMA((2, chains, n_row - 1)),
            pltpu.SemaphoreType.DMA((2, chains, n_row - 1)),
            pltpu.SemaphoreType.DMA((2, chains, n_col - 1)),
        ],
        compiler_params=pltpu.CompilerParams(
            collective_id=0, has_side_effects=True, vmem_limit_bytes=40 * 1024 * 1024
        ),
        cost_estimate=pl.CostEstimate(
            flops=4 * ITERS * n_con * n_var * cols_g * n_col,
            bytes_accessed=8 * 1024 * 1024,
            transcendentals=0,
        ),
    )(
        slot,
        mask,
        values,
        scenario_live.astype(F32)[None, :],
        turned(demand),
        path_cost[None, :],
        upper_bound[None, :],
        turned(primal_start),
        turned(dual_start),
    )
    return primal.reshape(rows_g, n_var).T, dual.reshape(cols_g, n_con).T


def solution(mesh):
    in_specs = (
        P(("inst", "row"), "col", None, None, None),
        P(("inst", "row"), "col", None),
        P(("inst", "row"), "col", None),
        P(("inst", "row"), "col"),
        P(("inst", "row")),
        P(("inst", "row"), "col"),
        P(("inst", "col")),
        P(("inst", "col")),
        P(("inst", "col"), "row"),
        P(("inst", "row"), "col"),
    )
    out_specs = (P(("inst", "col"), "row"), P(("inst", "row"), "col"))
    return jax.shard_map(
        functools.partial(on_device, mesh.shape["row"], mesh.shape["col"]),
        mesh=mesh,
        in_specs=in_specs,
        out_specs=out_specs,
        check_vma=False,
    )
```

```python
import functools

import jax
import jax.numpy as jnp
from jax import lax
from jax.experimental import pallas as pl
from jax.experimental.pallas import tpu as pltpu
from jax.sharding import PartitionSpec as P

ITERS = 4

primal_step = 0.4
dual_step = 0.4

MESH = pl.DeviceIdType.MESH
BF16 = jnp.bfloat16
F32 = jnp.float32


def kernel(
    n_row,
    n_col,
    chains,
    row_blocks,
    col_blocks,
    slot_ref,
    mask_ref,
    values_ref,
    live_ref,
    demand_ref,
    cost_ref,
    bound_ref,
    primal_in,
    dual_in,
    primal_ref,
    dual_ref,
    matrix,
    matrix_t,
    dual_all,
    lift_part,
    lift_out,
    lift_in,
    flow_all,
    load_part,
    load_out,
    load_in,
    dual_sems,
    lift_sems,
    flow_sems,
    load_sems,
):
    row = lax.axis_index("row")
    col = lax.axis_index("col")
    block = values_ref.shape[1]
    rows_g = primal_in.shape[1]
    cols_g = dual_in.shape[1]

    def peer(axis, d):
        me, n = (row, n_row) if axis == "row" else (col, n_col)
        return lax.rem(me + d, n)

    barrier = pltpu.get_barrier_semaphore()
    for axis, n in (("row", n_row), ("col", n_col)):
        for d in range(1, n):
            pl.semaphore_signal(
                barrier, inc=1, device_id={axis: peer(axis, d)}, device_id_type=MESH
            )

    def copies(axis, n, source, target, sems, h, gather):
        me = row if axis == "row" else col
        made = []
        for d in range(1, n):
            to = peer(axis, d)
            made.append(
                pltpu.make_async_remote_copy(
                    src_ref=source.at[h, me if gather else to],
                    dst_ref=target.at[h, me],
                    send_sem=sems.at[0, h, d - 1],
                    recv_sem=sems.at[1, h, d - 1],
                    device_id={axis: to},
                    device_id_type=MESH,
                )
            )
        return made

    dual_cp = [
        copies("col", n_col, dual_all, dual_all, dual_sems, h, True) for h in range(chains)
    ]
    lift_cp = [
        copies("row", n_row, lift_out, lift_in, lift_sems, h, False) for h in range(chains)
    ]
    flow_cp = [
        copies("row", n_row, flow_all, flow_all, flow_sems, h, True) for h in range(chains)
    ]
    load_cp = [
        copies("col", n_col, load_out, load_in, load_sems, h, False) for h in range(chains)
    ]

    def send(made):
        for one in made:
            one.start()

    def settle(made):
        for one in made:
            one.wait()

    for h in range(chains):
        primal_ref[h] = primal_in[h]
        dual_ref[h] = dual_in[h]
        dual_all[h, col] = dual_in[h].astype(BF16)
    pl.semaphore_wait(barrier, n_row + n_col - 2)
    for h in range(chains):
        send(dual_cp[h])

    for r in range(row_blocks):
        for c in range(col_blocks):
            at = r * col_blocks + c
            placed = values_ref[slot_ref[at]].astype(F32) * mask_ref[at]
            matrix[r * block : (r + 1) * block, c * block : (c + 1) * block] = placed.astype(BF16)
            matrix_t[c * block : (c + 1) * block, r * block : (r + 1) * block] = placed.T.astype(BF16)

    def lift(h):
        settle(dual_cp[h])
        source = dual_all[h].reshape(n_col * cols_g, matrix.shape[0])
        part = jnp.dot(source, matrix[...], preferred_element_type=F32)
        part = part.reshape(n_row, rows_g, matrix.shape[1])
        lift_part[h] = part
        lift_out[h] = part.astype(BF16)
        send(lift_cp[h])

    def move_primal(h):
        settle(lift_cp[h])
        lifted = lift_part[h, row]
        for d in range(1, n_row):
            lifted = lifted + lift_in[h, lax.rem(row + n_row - d, n_row)].astype(F32)
        primal = primal_ref[h]
        following = jnp.minimum(
            jnp.maximum(primal - primal_step * (cost_ref[...] - lifted), 0.0), bound_ref[...]
        )
        primal_ref[h] = following
        flow_all[h, row] = (2.0 * following - primal).astype(BF16)
        send(flow_cp[h])

    def load(h):
        settle(flow_cp[h])
        source = flow_all[h].reshape(n_row * rows_g, matrix.shape[1])
        part = jnp.dot(source, matrix_t[...], preferred_element_type=F32)
        part = part.reshape(n_col, cols_g, matrix.shape[0])
        load_part[h] = part
        load_out[h] = part.astype(BF16)
        send(load_cp[h])

    def move_dual(h, step):
        settle(load_cp[h])
        loads = load_part[h, col]
        for d in range(1, n_col):
            loads = loads + load_in[h, lax.rem(col + n_col - d, n_col)].astype(F32)
        dual = live_ref[...] * jnp.maximum(
            dual_ref[h] + dual_step * (demand_ref[h] - loads), 0.0
        )
        dual_ref[h] = dual
        dual_all[h, col] = dual.astype(BF16)

        @pl.when(step < ITERS - 1)
        def _():
            send(dual_cp[h])

    early = tuple(range((chains + 1) // 2))
    late = tuple(range((chains + 1) // 2, chains))

    def half(mine, others, step, others_step, first):
        for h in mine:
            lift(h)
        for h in mine:
            move_primal(h)
        for at in range(max(len(mine), len(others))):
            if at < len(others):
                if first:
                    pl.when(step > 0)(functools.partial(move_dual, others[at], others_step))
                else:
                    move_dual(others[at], others_step)
            if at < len(mine):
                load(mine[at])

    def one_step(step, carry):
        half(early, late, step, step - 1, True)
        half(late, early, step, step, False)
        return carry

    lax.fori_loop(0, ITERS, one_step, 0)
    for h in late:
        move_dual(h, jnp.int32(ITERS - 1))


def on_device(
    n_row,
    n_col,
    block_values,
    block_rows,
    block_cols,
    block_count,
    scenario_live,
    demand,
    path_cost,
    upper_bound,
    primal_start,
    dual_start,
):
    values = block_values[0, 0]
    slots, block_size = values.shape[0], values.shape[1]
    n_con, cols_g = dual_start.shape
    n_var, rows_g = primal_start.shape
    row_blocks = n_con // block_size
    col_blocks = n_var // block_size
    numbers = jnp.arange(slots, dtype=jnp.int32)
    place = block_rows[0, 0] * col_blocks + block_cols[0, 0]
    hit = (place[None, :] == jnp.arange(row_blocks * col_blocks, dtype=jnp.int32)[:, None]) & (
        numbers < block_count[0, 0]
    )[None, :]
    slot = jnp.sum(jnp.where(hit, numbers[None, :], 0), axis=1)
    mask = jnp.sum(jnp.where(hit, 1.0, 0.0), axis=1)

    chains = 2 if n_row == n_col and cols_g == rows_g and cols_g % 32 == 0 else 1
    cg, rg = cols_g // chains, rows_g // chains

    def turned(array):
        return array.T.reshape(chains, array.shape[1] // chains, array.shape[0])

    vmem = pl.BlockSpec(memory_space=pltpu.VMEM)
    smem = pl.BlockSpec(memory_space=pltpu.SMEM)
    primal, dual = pl.pallas_call(
        functools.partial(kernel, n_row, n_col, chains, row_blocks, col_blocks),
        out_shape=(
            jax.ShapeDtypeStruct((chains, rg, n_var), F32),
            jax.ShapeDtypeStruct((chains, cg, n_con), F32),
        ),
        in_specs=[smem, smem] + [vmem] * 7,
        out_specs=(vmem, vmem),
        scratch_shapes=[
            pltpu.VMEM((n_con, n_var), BF16),
            pltpu.VMEM((n_var, n_con), BF16),
            pltpu.VMEM((chains, n_col, cg, n_con), BF16),
            pltpu.VMEM((chains, n_row, rg, n_var), F32),
            pltpu.VMEM((chains, n_row, rg, n_var), BF16),
            pltpu.VMEM((chains, n_row, rg, n_var), BF16),
            pltpu.VMEM((chains, n_row, rg, n_var), BF16),
            pltpu.VMEM((chains, n_col, cg, n_con), F32),
            pltpu.VMEM((chains, n_col, cg, n_con), BF16),
            pltpu.VMEM((chains, n_col, cg, n_con), BF16),
            pltpu.SemaphoreType.DMA((2, chains, n_col - 1)),
            pltpu.SemaphoreType.DMA((2, chains, n_row - 1)),
            pltpu.SemaphoreType.DMA((2, chains, n_row - 1)),
            pltpu.SemaphoreType.DMA((2, chains, n_col - 1)),
        ],
        compiler_params=pltpu.CompilerParams(
            collective_id=0, has_side_effects=True, vmem_limit_bytes=40 * 1024 * 1024
        ),
        cost_estimate=pl.CostEstimate(
            flops=4 * ITERS * n_con * n_var * cols_g * n_col,
            bytes_accessed=8 * 1024 * 1024,
            transcendentals=0,
        ),
    )(
        slot,
        mask,
        values,
        scenario_live.astype(F32)[None, :],
        turned(demand),
        path_cost[None, :],
        upper_bound[None, :],
        turned(primal_start),
        turned(dual_start),
    )
    return primal.reshape(rows_g, n_var).T, dual.reshape(cols_g, n_con).T


def solution(mesh):
    in_specs = (
        P(("inst", "row"), "col", None, None, None),
        P(("inst", "row"), "col", None),
        P(("inst", "row"), "col", None),
        P(("inst", "row"), "col"),
        P(("inst", "row")),
        P(("inst", "row"), "col"),
        P(("inst", "col")),
        P(("inst", "col")),
        P(("inst", "col"), "row"),
        P(("inst", "row"), "col"),
    )
    out_specs = (P(("inst", "col"), "row"), P(("inst", "row"), "col"))
    return jax.shard_map(
        functools.partial(on_device, mesh.shape["row"], mesh.shape["col"]),
        mesh=mesh,
        in_specs=in_specs,
        out_specs=out_specs,
        check_vma=False,
    )
```

```python
import functools

import jax
import jax.numpy as jnp
from jax import lax
from jax.experimental import pallas as pl
from jax.experimental.pallas import tpu as pltpu
from jax.sharding import PartitionSpec as P

ITERS = 4

primal_step = 0.4
dual_step = 0.4

MESH = pl.DeviceIdType.MESH
BF16 = jnp.bfloat16
F32 = jnp.float32


def kernel(
    n_row,
    n_col,
    chains,
    row_blocks,
    col_blocks,
    slot_ref,
    mask_ref,
    values_in,
    live_in,
    demand_in,
    cost_in,
    bound_in,
    primal_in,
    dual_in,
    primal_ref,
    dual_ref,
    values_ref,
    live_ref,
    demand_ref,
    cost_ref,
    bound_ref,
    matrix,
    matrix_t,
    dual_all,
    lift_part,
    lift_out,
    lift_in,
    flow_all,
    load_part,
    load_out,
    load_in,
    dual_sems,
    lift_sems,
    flow_sems,
    load_sems,
    stage_sems,
):
    staged = (
        (dual_in, dual_ref),
        (values_in, values_ref),
        (primal_in, primal_ref),
        (cost_in, cost_ref),
        (bound_in, bound_ref),
        (demand_in, demand_ref),
        (live_in, live_ref),
    )
    stage_cp = [
        pltpu.make_async_copy(source, target, stage_sems.at[at])
        for at, (source, target) in enumerate(staged)
    ]
    for one in stage_cp:
        one.start()
    row = lax.axis_index("row")
    col = lax.axis_index("col")
    block = values_ref.shape[1]
    rows_g = primal_in.shape[1]
    cols_g = dual_in.shape[1]

    def peer(axis, d):
        me, n = (row, n_row) if axis == "row" else (col, n_col)
        return lax.rem(me + d, n)

    barrier = pltpu.get_barrier_semaphore()
    for axis, n in (("row", n_row), ("col", n_col)):
        for d in range(1, n):
            pl.semaphore_signal(
                barrier, inc=1, device_id={axis: peer(axis, d)}, device_id_type=MESH
            )

    def copies(axis, n, source, target, sems, h, gather):
        me = row if axis == "row" else col
        made = []
        for d in range(1, n):
            to = peer(axis, d)
            made.append(
                pltpu.make_async_remote_copy(
                    src_ref=source.at[h, me if gather else to],
                    dst_ref=target.at[h, me],
                    send_sem=sems.at[0, h, d - 1],
                    recv_sem=sems.at[1, h, d - 1],
                    device_id={axis: to},
                    device_id_type=MESH,
                )
            )
        return made

    dual_cp = [
        copies("col", n_col, dual_all, dual_all, dual_sems, h, True) for h in range(chains)
    ]
    lift_cp = [
        copies("row", n_row, lift_out, lift_in, lift_sems, h, False) for h in range(chains)
    ]
    flow_cp = [
        copies("row", n_row, flow_all, flow_all, flow_sems, h, True) for h in range(chains)
    ]
    load_cp = [
        copies("col", n_col, load_out, load_in, load_sems, h, False) for h in range(chains)
    ]

    def send(made):
        for one in made[::2] + made[1::2]:
            one.start()

    def settle(made):
        for one in made:
            one.wait()

    stage_cp[0].wait()
    for h in range(chains):
        dual_all[h, col] = dual_ref[h].astype(BF16)
    pl.semaphore_wait(barrier, n_row + n_col - 2)
    for h in range(chains):
        send(dual_cp[h])

    stage_cp[1].wait()
    for r in range(row_blocks):
        for c in range(col_blocks):
            at = r * col_blocks + c
            placed = values_ref[slot_ref[at]].astype(F32) * mask_ref[at]
            matrix[r * block : (r + 1) * block, c * block : (c + 1) * block] = placed.astype(BF16)
            matrix_t[c * block : (c + 1) * block, r * block : (r + 1) * block] = placed.T.astype(BF16)

    for one in stage_cp[2:]:
        one.wait()

    def lift(h):
        settle(dual_cp[h])
        source = dual_all[h].reshape(n_col * cols_g, matrix.shape[0])
        part = jnp.dot(source, matrix[...], preferred_element_type=F32)
        part = part.reshape(n_row, rows_g, matrix.shape[1])
        lift_part[h] = part
        lift_out[h] = part.astype(BF16)
        send(lift_cp[h])

    def move_primal(h):
        settle(lift_cp[h])
        lifted = lift_part[h, row]
        for d in range(1, n_row):
            lifted = lifted + lift_in[h, lax.rem(row + n_row - d, n_row)].astype(F32)
        primal = primal_ref[h]
        following = jnp.minimum(
            jnp.maximum(primal - primal_step * (cost_ref[...] - lifted), 0.0), bound_ref[...]
        )
        primal_ref[h] = following
        flow_all[h, row] = (2.0 * following - primal).astype(BF16)
        send(flow_cp[h])

    def load(h):
        settle(flow_cp[h])
        source = flow_all[h].reshape(n_row * rows_g, matrix.shape[1])
        part = jnp.dot(source, matrix_t[...], preferred_element_type=F32)
        part = part.reshape(n_col, cols_g, matrix.shape[0])
        load_part[h] = part
        load_out[h] = part.astype(BF16)
        send(load_cp[h])

    def move_dual(h, step):
        settle(load_cp[h])
        loads = load_part[h, col]
        for d in range(1, n_col):
            loads = loads + load_in[h, lax.rem(col + n_col - d, n_col)].astype(F32)
        dual = live_ref[...].astype(F32) * jnp.maximum(
            dual_ref[h] + dual_step * (demand_ref[h] - loads), 0.0
        )
        dual_ref[h] = dual
        dual_all[h, col] = dual.astype(BF16)

        @pl.when(step < ITERS - 1)
        def _():
            send(dual_cp[h])

    early = tuple(range((chains + 1) // 2))
    late = tuple(range((chains + 1) // 2, chains))

    def half(mine, others, step, others_step, first):
        for h in mine:
            lift(h)
        for h in others:
            if first:
                pl.when(step > 0)(functools.partial(move_dual, h, others_step))
            else:
                move_dual(h, others_step)
        for h in mine:
            move_primal(h)
        for h in mine:
            load(h)

    def one_step(step, carry):
        half(early, late, step, step - 1, True)
        half(late, early, step, step, False)
        return carry

    lax.fori_loop(0, ITERS, one_step, 0)
    for h in late:
        move_dual(h, jnp.int32(ITERS - 1))


def on_device(
    n_row,
    n_col,
    block_values,
    block_rows,
    block_cols,
    block_count,
    scenario_live,
    demand,
    path_cost,
    upper_bound,
    primal_start,
    dual_start,
):
    values = block_values[0, 0]
    slots, block_size = values.shape[0], values.shape[1]
    n_con, cols_g = dual_start.shape
    n_var, rows_g = primal_start.shape
    row_blocks = n_con // block_size
    col_blocks = n_var // block_size
    numbers = jnp.arange(slots, dtype=jnp.int32)
    place = block_rows[0, 0] * col_blocks + block_cols[0, 0]
    hit = (place[None, :] == jnp.arange(row_blocks * col_blocks, dtype=jnp.int32)[:, None]) & (
        numbers < block_count[0, 0]
    )[None, :]
    slot = jnp.sum(jnp.where(hit, numbers[None, :], 0), axis=1)
    mask = jnp.sum(jnp.where(hit, 1.0, 0.0), axis=1)

    chains = 2 if n_row == n_col and cols_g == rows_g and cols_g % 32 == 0 else 1
    cg, rg = cols_g // chains, rows_g // chains

    def turned(array):
        return array.T.reshape(chains, array.shape[1] // chains, array.shape[0])

    vmem = pl.BlockSpec(memory_space=pltpu.VMEM)
    smem = pl.BlockSpec(memory_space=pltpu.SMEM)
    primal, dual = pl.pallas_call(
        functools.partial(kernel, n_row, n_col, chains, row_blocks, col_blocks),
        out_shape=(
            jax.ShapeDtypeStruct((chains, rg, n_var), F32),
            jax.ShapeDtypeStruct((chains, cg, n_con), F32),
        ),
        in_specs=[smem, smem] + [pl.BlockSpec(memory_space=pl.ANY)] * 7,
        out_specs=(vmem, vmem),
        scratch_shapes=[
            pltpu.VMEM(values.shape, BF16),
            pltpu.VMEM((1, n_con), jnp.int32),
            pltpu.VMEM((chains, cg, n_con), F32),
            pltpu.VMEM((1, n_var), F32),
            pltpu.VMEM((1, n_var), F32),
            pltpu.VMEM((n_con, n_var), BF16),
            pltpu.VMEM((n_var, n_con), BF16),
            pltpu.VMEM((chains, n_col, cg, n_con), BF16),
            pltpu.VMEM((chains, n_row, rg, n_var), F32),
            pltpu.VMEM((chains, n_row, rg, n_var), BF16),
            pltpu.VMEM((chains, n_row, rg, n_var), BF16),
            pltpu.VMEM((chains, n_row, rg, n_var), BF16),
            pltpu.VMEM((chains, n_col, cg, n_con), F32),
            pltpu.VMEM((chains, n_col, cg, n_con), BF16),
            pltpu.VMEM((chains, n_col, cg, n_con), BF16),
            pltpu.SemaphoreType.DMA((2, chains, n_col - 1)),
            pltpu.SemaphoreType.DMA((2, chains, n_row - 1)),
            pltpu.SemaphoreType.DMA((2, chains, n_row - 1)),
            pltpu.SemaphoreType.DMA((2, chains, n_col - 1)),
            pltpu.SemaphoreType.DMA((7,)),
        ],
        compiler_params=pltpu.CompilerParams(
            collective_id=0, has_side_effects=True, vmem_limit_bytes=56 * 1024 * 1024
        ),
        cost_estimate=pl.CostEstimate(
            flops=4 * ITERS * n_con * n_var * cols_g * n_col,
            bytes_accessed=8 * 1024 * 1024,
            transcendentals=0,
        ),
    )(
        slot,
        mask,
        values,
        scenario_live[None, :],
        turned(demand),
        path_cost[None, :],
        upper_bound[None, :],
        turned(primal_start),
        turned(dual_start),
    )
    return primal.reshape(rows_g, n_var).T, dual.reshape(cols_g, n_con).T


def solution(mesh):
    in_specs = (
        P(("inst", "row"), "col", None, None, None),
        P(("inst", "row"), "col", None),
        P(("inst", "row"), "col", None),
        P(("inst", "row"), "col"),
        P(("inst", "row")),
        P(("inst", "row"), "col"),
        P(("inst", "col")),
        P(("inst", "col")),
        P(("inst", "col"), "row"),
        P(("inst", "row"), "col"),
    )
    out_specs = (P(("inst", "col"), "row"), P(("inst", "row"), "col"))
    return jax.shard_map(
        functools.partial(on_device, mesh.shape["row"], mesh.shape["col"]),
        mesh=mesh,
        in_specs=in_specs,
        out_specs=out_specs,
        check_vma=False,
    )
```
